128 devices in a mesh: row: 16 (over z_hi, y, core), col: 8 (over x, z_lo).
Axes of the slice: x: 4, y: 4, z: 4 (z_hi: 2, z_lo: 2; z = z_hi * 2 + z_lo), core: 2. Of those that a mesh axis runs over, the one named last changes fastest.
Arguments:
- features: bfloat16 [131072, 128], P(('row', 'col')), may hold values from -6 to 6
- block_rows: int32 [16, 8, 704], P('row', 'col'), may hold values from 0 to 63, as said below
- block_cols: int32 [16, 8, 704], P('row', 'col'), may hold values from 0 to 127
- block_vals: bfloat16 [16, 8, 704, 128, 128], P('row', 'col'), may hold values from -0.0546875 to 0.0546875
- tile_counts: int32 [16, 8], P('row', 'col'), may hold values from 88 to 704
- w_first: bfloat16 [128, 128], replicated, may hold values from -0.5 to 0.5
- b_first: float32 [128], replicated, may hold values from -3 to 3
- w_second: bfloat16 [128, 128], replicated, may hold values from -0.5 to 0.5
- b_second: float32 [128], replicated, may hold values from -3 to 3
Outputs:
- node_out: bfloat16 [131072, 128], P(('row', 'col'))
The draws below stay inside these ranges and needn't reach their ends.
Inputs may be any that keep to these rules, and one draw needn't show every extreme that they name: Within one tile the pairs (block_rows, block_cols) of all 704 slots are distinct.
All inputs are finite; a program needn't handle non-finite values.
Results may differ from the reference program's by a relative error of at most 0.02.
Values may be sent and summed in bfloat16 or wider, within the bound.
A program may use at most 192 MiB of HBM per device.

```python
import jax
import jax.numpy as jnp
from jax import lax

F = 128
BS = 128
BPD = 8
KMAX = 704
NODES = 131072
N_ROW = 16
N_COL = 8


def tile_positions(key):
    tiles = N_ROW * N_COL
    places = N_COL * BPD * (N_ROW * BPD)
    pick_keys = jax.random.split(jax.random.fold_in(key, 1), tiles)
    order_keys = jax.random.split(jax.random.fold_in(key, 2), tiles)

    def one_tile(pick_key, order_key):
        middle = 1 + jax.random.permutation(pick_key, places - 2)[:KMAX - 2]
        listed = jnp.concatenate([jnp.array([0, places - 1], jnp.int32), middle.astype(jnp.int32)])
        order = jax.random.permutation(order_key, KMAX)
        return listed[order]
    return jax.vmap(one_tile)(pick_keys, order_keys).reshape(N_ROW, N_COL, KMAX)


def draw_block_rows(key, part):
    positions = tile_positions(key)
    return (positions // (N_ROW * BPD)).astype(jnp.int32)


def draw_block_cols(key, part):
    positions = tile_positions(key)
    return (positions % (N_ROW * BPD)).astype(jnp.int32)


def draw_tile_counts(key, part):
    key = jax.random.fold_in(key, 7)
    first, second = jax.random.split(key)
    levels = jax.random.randint(first, (N_ROW * N_COL,), 0, 28)
    chosen = jax.random.randint(second, (), 0, N_ROW * N_COL)
    levels = jnp.where(jnp.arange(N_ROW * N_COL) == chosen, 27, levels)
    counts = KMAX // 8 + (KMAX - KMAX // 8) * levels * levels // 729
    return counts.astype(jnp.int32).reshape(N_ROW, N_COL)


def steps_of(stream_key, extent, pieces, smallest, top_value):
    factor_of = 1.0
    for position, shards_of in pieces:
        heights = jax.random.uniform(jax.random.fold_in(jax.random.fold_in(stream_key, 6), position), (shards_of,), jnp.float32, smallest / len(pieces), top_value / len(pieces))
        factor_of = factor_of * jnp.repeat(jnp.exp(heights), extent[position] // shards_of).reshape((-1,) + (1,) * (len(extent) - 1 - position))
    return factor_of


def normal_values(key, dims, spread, most, pieces=(), kind=jnp.bfloat16):
    drawn = jax.random.normal(key, dims, jnp.float32) * spread
    if len(pieces) > 0:
        drawn = steps_of(key, dims, pieces, -0.22, 0.18) * drawn
    return jnp.clip(drawn, min=-most, max=most).astype(kind)


def setup_inputs(seed: int = 0) -> dict:
    keys = jax.random.split(jax.random.key(seed), 10)
    return {
        "features": normal_values(keys[0], (NODES, F), 1.0, 6.0, ((0, 128),)),
        "block_rows": draw_block_rows(jax.random.fold_in(keys[9], 71), 0),
        "block_cols": draw_block_cols(jax.random.fold_in(keys[9], 71), 0),
        "block_vals": normal_values(keys[3], (N_ROW, N_COL, KMAX, BS, BS), (BS * KMAX // BPD) ** -0.5, 0.0546875, ((0, 16), (1, 8))),
        "tile_counts": draw_tile_counts(jax.random.fold_in(keys[9], 71), 0),
        "w_first": normal_values(keys[5], (F, F), F ** -0.5, 0.5),
        "b_first": normal_values(keys[6], (F,), 0.5, 3.0, (), jnp.float32),
        "w_second": normal_values(keys[7], (F, F), F ** -0.5, 0.5),
        "b_second": normal_values(keys[8], (F,), 0.5, 3.0, (), jnp.float32),
    }


def aggregate(inputs, vals_flat, rows_flat, cols_flat, counts_flat):
    tiles = N_ROW * N_COL
    group_blocks = N_COL * BPD
    blocks = inputs.reshape(NODES // BS, BS, F)

    def visit(tile, total):
        row_group = tile // N_COL
        col_group = tile % N_COL
        local_rows = rows_flat[tile].astype(jnp.int32)
        local_cols = cols_flat[tile]
        global_cols = (((local_cols // BPD) * N_COL + col_group) * BPD + local_cols % BPD).astype(jnp.int32)
        picked = blocks[global_cols].astype(jnp.float32)
        product = jnp.einsum("kab,kbf->kaf", vals_flat[tile].astype(jnp.float32), picked)
        keep = jnp.arange(KMAX, dtype=jnp.int32) < counts_flat[tile]
        product = jnp.where(keep[:, None, None], product, 0.0)
        tile_total = jnp.zeros((group_blocks, BS, F), jnp.float32).at[local_rows].add(product)
        rounded = lax.optimization_barrier(tile_total.astype(jnp.bfloat16)).astype(jnp.float32)
        start = (row_group * group_blocks).astype(jnp.int32)
        zero = jnp.zeros((), jnp.int32)
        current = lax.dynamic_slice(total, (start, zero, zero), (group_blocks, BS, F))
        return lax.dynamic_update_slice(total, current + rounded, (start, zero, zero))

    total = lax.fori_loop(0, tiles, visit, jnp.zeros((NODES // BS, BS, F), jnp.float32))
    return total.reshape(NODES, F).astype(jnp.bfloat16)


def reference(features, block_rows, block_cols, block_vals, tile_counts, w_first, b_first, w_second, b_second):
    tiles = N_ROW * N_COL
    vals_flat = block_vals.reshape(tiles, KMAX, BS, BS)
    rows_flat = block_rows.reshape(tiles, KMAX)
    cols_flat = block_cols.reshape(tiles, KMAX)
    counts_flat = tile_counts.reshape(tiles)
    first_agg = aggregate(features, vals_flat, rows_flat, cols_flat, counts_flat)
    hidden = jax.nn.relu(jnp.dot(first_agg, w_first, preferred_element_type=jnp.float32) + b_first).astype(jnp.bfloat16)
    second_agg = aggregate(hidden, vals_flat, rows_flat, cols_flat, counts_flat)
    return (jnp.dot(second_agg, w_second, preferred_element_type=jnp.float32) + b_second).astype(jnp.bfloat16)
```

```python
import functools

import jax
import jax.numpy as jnp
from jax import lax
from jax.experimental import pallas as pl
from jax.experimental.pallas import tpu as pltpu
from jax.sharding import PartitionSpec as P

UNROLL = 64
LOADS = 8
LANES = 128
RING = 4
ROUNDS_FIRST = 2
ROUNDS_MIDDLE = 2
ROUNDS_LAST = 2


def halves(rounds, own_blocks):
    size = own_blocks // 2 // rounds
    return [
        ((i * size, size), (own_blocks // 2 + i * size, size)) for i in range(rounds)
    ]


def kernel(
    feat,
    rows_ref,
    cols_ref,
    vals_hbm,
    count_ref,
    w1,
    b1,
    w2,
    b2,
    out_ref,
    vals,
    sums,
    panel_one,
    panel_two,
    send_buf,
    far_buf,
    near_buf,
    plane_buf,
    pad_rows,
    pad_cols,
    list_v,
    list_s,
    load_sem,
    local_sem,
    send_sem,
    recv_sem,
):
    slots, bs, ch = vals.shape
    panels = (panel_one, panel_two)
    own_blocks = feat.shape[0]
    row_blocks = send_buf.shape[0]
    row = lax.axis_index("row")
    col = lax.axis_index("col")
    zh, y, core = row // 8, (row // 2) % RING, row % 2
    x, zl = col // 2, col % 2

    def row_of(dz, dy, dk):
        return ((zh + dz) % 2) * 8 + ((y + dy + RING) % RING) * 2 + (core + dk) % 2

    def col_of(dx, dl):
        return ((x + dx + RING) % RING) * 2 + (zl + dl) % 2

    yp, ym = (row_of(0, 1, 0), col), (row_of(0, -1, 0), col)
    zp, sib = (row_of(1, 0, 0), col), (row_of(0, 0, 1), col)
    xp, xm, lp = (row, col_of(1, 0)), (row, col_of(-1, 0)), (row, col_of(0, 1))

    loads = []
    share = slots // LOADS
    for i in range(LOADS):
        part = pl.ds(i * share, share)
        loads.append(pltpu.make_async_copy(vals_hbm.at[part], vals.at[part], load_sem.at[i]))
        loads[-1].start()
    own_copy = pltpu.make_async_copy(
        feat, panel_one.at[pl.ds(row * own_blocks, own_blocks)], local_sem.at[0]
    )
    own_copy.start()

    barrier = pltpu.get_barrier_semaphore()
    for peer in (yp, ym, zp, sib, xp, xm, lp):
        pl.semaphore_signal(barrier, inc=1, device_id=peer, device_id_type=pl.DeviceIdType.MESH)
    pl.semaphore_wait(barrier, 7)

    started = []

    def send(src, dst, peer):
        i = len(started)
        copy = pltpu.make_async_remote_copy(
            src_ref=src,
            dst_ref=dst,
            send_sem=send_sem.at[i],
            recv_sem=recv_sem.at[i],
            device_id=peer,
            device_id_type=pl.DeviceIdType.MESH,
        )
        copy.start()
        started.append(copy)
        return copy

    def gather_round(layer, pair, own_src):
        def at(who, piece):
            return panels[layer].at[pl.ds(who * own_blocks + piece[0], piece[1])]

        def forward(who, piece, peer):
            return send(at(who, piece), at(who, piece), peer)

        a, b = pair
        me = row
        up = {p: send(own_src(p), at(me, p), yp) for p in pair}
        down = {p: send(own_src(p), at(me, p), ym) for p in pair}
        over = {p: send(own_src(p), at(me, p), zp) for p in pair}
        shared = [send(own_src(p), at(me, p), sib) for p in pair]
        yield
        below, above, across = row_of(0, -1, 0), row_of(0, 1, 0), row_of(1, 0, 0)
        up[a].wait_recv()
        up_a = forward(below, a, yp)
        down[b].wait_recv()
        down_b = forward(above, b, ym)
        over_up, over_down = {}, {}
        for p in pair:
            over[p].wait_recv()
            over_up[p] = forward(across, p, yp)
            over_down[p] = forward(across, p, ym)
        up[b].wait_recv()
        down[a].wait_recv()
        for who in (below, above, across):
            for p in pair:
                shared.append(forward(who, p, sib))
        yield
        below2, above2 = row_of(1, -1, 0), row_of(1, 1, 0)
        far, far2 = row_of(0, 2, 0), row_of(1, 2, 0)
        over_up[a].wait_recv()
        up_a2 = forward(below2, a, yp)
        over_down[b].wait_recv()
        down_b2 = forward(above2, b, ym)
        up_a.wait_recv()
        shared.append(forward(far, a, sib))
        down_b.wait_recv()
        shared.append(forward(far, b, sib))
        over_up[b].wait_recv()
        over_down[a].wait_recv()
        for who in (below2, above2):
            for p in pair:
                shared.append(forward(who, p, sib))
        yield
        up_a2.wait_recv()
        shared.append(forward(far2, a, sib))
        down_b2.wait_recv()
        shared.append(forward(far2, b, sib))
        yield
        for copy in shared:
            copy.wait_recv()
        yield

    def build_lists():
        tiles = pad_rows.shape[0]
        lane = lax.broadcasted_iota(jnp.int32, (LANES, LANES), 1)
        depth = lax.broadcasted_iota(jnp.int32, (LANES, LANES), 0)
        place = lax.broadcasted_iota(jnp.int32, (1, LANES), 1)
        live_count = count_ref[0, 0]
        for t in range(tiles):
            width = min(LANES, slots - t * LANES)
            if width < LANES:
                pad_rows[t : t + 1, :] = jnp.zeros((1, LANES), jnp.int32)
                pad_cols[t : t + 1, :] = jnp.zeros((1, LANES), jnp.int32)
            pad_rows[t : t + 1, 0:width] = rows_ref[0, :, t * LANES : t * LANES + width]
            pad_cols[t : t + 1, 0:width] = cols_ref[0, :, t * LANES : t * LANES + width]
        key_rows, key_cols, load_cols, group_cols = [], [], [], []

        def upright(v):
            return jnp.sum(jnp.where(lane == depth, v, 0), axis=1, keepdims=True)

        for t in range(tiles):
            index = place + t * LANES
            group = jnp.where(index < live_count, pad_rows[t : t + 1, :], LANES - 1)
            key = group * 1024 + index
            key_rows.append(key)
            key_cols.append(upright(key))
            load_cols.append(upright(index + pad_cols[t : t + 1, :] * 1024 + group * 131072))
            group_cols.append(upright(group))
        ranks = []
        for t in range(tiles):
            below = jnp.zeros((LANES, LANES), jnp.int32)
            for s in range(tiles):
                below = below + (key_rows[s] < key_cols[t]).astype(jnp.int32)
            ranks.append(jnp.sum(below, axis=1, keepdims=True))
        for t in range(tiles):
            found = jnp.zeros((LANES, LANES), jnp.int32)
            for s in range(tiles):
                found = found + jnp.where(ranks[s] == lane + t * LANES, load_cols[s], 0)
            list_v[t : t + 1, :] = jnp.sum(found, axis=0, keepdims=True)
        upto = jnp.zeros((LANES, LANES), jnp.int32)
        for s in range(tiles):
            upto = upto + (group_cols[s] <= lane).astype(jnp.int32)
        list_v[tiles : tiles + 1, :] = jnp.sum(upto, axis=0, keepdims=True)
        for t in range(tiles + 1, list_v.shape[0]):
            list_v[t : t + 1, :] = jnp.zeros((1, LANES), jnp.int32)
        copy = pltpu.make_async_copy(list_v, list_s, local_sem.at[1])
        copy.start()
        copy.wait()

    def multiply(layer):
        halves_per_row = LANES // UNROLL

        def group(g, carry):
            total, last = carry
            for u in range(UNROLL):
                entry = list_s[g // halves_per_row, (g % halves_per_row) * UNROLL + u]
                slot = entry & 1023
                source = (entry >> 10) & 127
                target = entry >> 17
                product = jnp.dot(
                    vals[slot], panels[layer][source], preferred_element_type=jnp.float32
                )
                total = jnp.where(target == last, total, 0.0) + product
                sums[g * UNROLL + u] = total.astype(jnp.bfloat16)
                last = target
            return total, last

        lax.fori_loop(
            0, slots // UNROLL, group, (jnp.zeros((bs, ch), jnp.float32), jnp.int32(-1))
        )

    tiles = pad_rows.shape[0]

    def collect(owner):
        for j in range(own_blocks):
            r = owner * own_blocks + j
            end = list_s[tiles, r]
            start = jnp.where(r > 0, list_s[tiles, jnp.maximum(r - 1, 0)], 0)
            value = sums[jnp.maximum(end - 1, 0)]
            send_buf[r] = jnp.where(end > start, value, jnp.zeros_like(value))

    def wide(v):
        return v.astype(jnp.float32)

    def scatter(layer, pairs, finish, after):
        for dx in (2, 1, -1, 0):
            for dl in (1, 0):
                collect(col_of(dx, dl))

        def part(dx, dl, piece):
            return send_buf.at[pl.ds(col_of(dx, dl) * own_blocks + piece[0], piece[1])]

        half = own_blocks // 2

        def first(i):
            a, b = pairs[i]
            far, near = {}, {}
            for dl in (1, 0):
                far[dl] = (
                    send(part(2, dl, a), far_buf.at[layer, 0, dl, pl.ds(a[0], a[1])], xp),
                    send(part(2, dl, b), far_buf.at[layer, 1, dl, pl.ds(b[0] - half, b[1])], xm),
                )
            for dl in (1, 0):
                near[dl] = [
                    send(part(1, dl, b), near_buf.at[layer, 0, dl, pl.ds(b[0], b[1])], xp),
                    send(part(-1, dl, a), near_buf.at[layer, 1, dl, pl.ds(a[0], a[1])], xm),
                ]
            return far, near

        def second(i, far, near):
            a, b = pairs[i]
            for dl in (1, 0):
                far[dl][0].wait_recv()
                mine = part(1, dl, a)
                mine[...] = (
                    wide(mine[...]) + wide(far_buf[layer, 0, dl, a[0] : a[0] + a[1]])
                ).astype(jnp.bfloat16)
                near[dl].append(
                    send(mine, near_buf.at[layer, 0, dl, pl.ds(a[0], a[1])], xp)
                )
                far[dl][1].wait_recv()
                mine = part(-1, dl, b)
                mine[...] = (
                    wide(mine[...])
                    + wide(far_buf[layer, 1, dl, b[0] - half : b[0] - half + b[1]])
                ).astype(jnp.bfloat16)
                near[dl].append(
                    send(mine, near_buf.at[layer, 1, dl, pl.ds(b[0], b[1])], xm)
                )

        def summed(dl, p):
            return (
                wide(part(0, dl, p)[...])
                + wide(near_buf[layer, 0, dl, p[0] : p[0] + p[1]])
                + wide(near_buf[layer, 1, dl, p[0] : p[0] + p[1]])
            )

        def third(i, near):
            planes = []
            for copy in near[1]:
                copy.wait_recv()
            for p in pairs[i]:
                mine = part(0, 1, p)
                mine[...] = summed(1, p).astype(jnp.bfloat16)
                planes.append(send(mine, plane_buf.at[layer, pl.ds(p[0], p[1])], lp))
            return planes

        def fourth(i, near, planes):
            for copy in near[0]:
                copy.wait_recv()
            for p, copy in zip(pairs[i], planes):
                copy.wait_recv()
                total = summed(0, p) + wide(plane_buf[layer, p[0] : p[0] + p[1]])
                finish(p, total.astype(jnp.bfloat16).reshape(p[1] * bs, ch))

        state = first(0)
        for i in range(len(pairs)):
            far, near = state
            second(i, far, near)
            if i + 1 < len(pairs):
                state = first(i + 1)
            planes = third(i, near)
            fourth(i, near, planes)
            after(i)

    pairs = halves(ROUNDS_FIRST, own_blocks)
    rounds = [
        gather_round(0, pair, lambda p: feat.at[pl.ds(p[0], p[1])]) for pair in pairs
    ]
    for r in rounds:
        next(r)
    build_lists()
    for _ in range(4):
        for r in rounds:
            next(r)
    own_copy.wait()
    for copy in loads:
        copy.wait()
    multiply(0)

    middle = halves(ROUNDS_MIDDLE, own_blocks)
    live = []

    def hidden(p, agg):
        value = jnp.dot(agg, w1[...], preferred_element_type=jnp.float32) + b1[...]
        value = jnp.maximum(value, 0.0).astype(jnp.bfloat16)
        panel_two[pl.ds(row * own_blocks + p[0], p[1])] = value.reshape(p[1], bs, ch)

    def own_hidden(p):
        return panel_two.at[pl.ds(row * own_blocks + p[0], p[1])]

    def step_all():
        for r in live:
            next(r)

    def after(i):
        step_all()
        live.append(gather_round(1, middle[i], own_hidden))
        next(live[-1])

    before = len(started)
    scatter(0, middle, hidden, after)
    stages = {id(r): len(middle) - i for i, r in enumerate(live)}
    while live:
        for r in list(live):
            if stages[id(r)] == 5:
                live.remove(r)
            else:
                next(r)
                stages[id(r)] += 1
    multiply(1)

    for copy in started[before:]:
        copy.wait_send()

    def final(p, agg):
        value = jnp.dot(agg, w2[...], preferred_element_type=jnp.float32) + b2[...]
        out_ref[p[0] : p[0] + p[1]] = value.astype(jnp.bfloat16).reshape(p[1], bs, ch)

    tail = len(started)
    scatter(1, halves(ROUNDS_LAST, own_blocks), final, lambda i: None)
    for copy in started[:before] + started[tail:]:
        copy.wait_send()


def count_copies():
    gather, scatter_ = 30, 14
    return gather * (ROUNDS_FIRST + ROUNDS_MIDDLE) + scatter_ * (ROUNDS_MIDDLE + ROUNDS_LAST)


def per_device(
    features, block_rows, block_cols, block_vals, tile_counts, w_first, b_first, w_second, b_second
):
    slots, bs = block_vals.shape[2], block_vals.shape[3]
    ch = features.shape[1]
    own_blocks = features.shape[0] // bs
    n_row, n_col = lax.axis_size("row"), lax.axis_size("col")
    panel_blocks = n_row * own_blocks
    row_blocks = n_col * own_blocks
    tiles = -(-slots // LANES)
    half = own_blocks // 2
    bf16 = jnp.bfloat16
    copies = count_copies()
    vmem = pl.BlockSpec(memory_space=pltpu.VMEM)
    hbm = pl.BlockSpec(memory_space=pl.ANY)
    out = pl.pallas_call(
        kernel,
        out_shape=jax.ShapeDtypeStruct((own_blocks, bs, ch), bf16),
        in_specs=[hbm, vmem, vmem, hbm, pl.BlockSpec(memory_space=pltpu.SMEM)] + [vmem] * 4,
        out_specs=vmem,
        scratch_shapes=[
            pltpu.VMEM((slots, bs, bs), bf16),
            pltpu.VMEM((slots, bs, ch), bf16),
            pltpu.VMEM((panel_blocks, bs, ch), bf16),
            pltpu.VMEM((panel_blocks, bs, ch), bf16),
            pltpu.VMEM((row_blocks, bs, ch), bf16),
            pltpu.VMEM((2, 2, 2, half, bs, ch), bf16),
            pltpu.VMEM((2, 2, 2, own_blocks, bs, ch), bf16),
            pltpu.VMEM((2, own_blocks, bs, ch), bf16),
            pltpu.VMEM((tiles, LANES), jnp.int32),
            pltpu.VMEM((tiles, LANES), jnp.int32),
            pltpu.VMEM((8, LANES), jnp.int32),
            pltpu.SMEM((8, LANES), jnp.int32),
            pltpu.SemaphoreType.DMA((LOADS,)),
            pltpu.SemaphoreType.DMA((2,)),
            pltpu.SemaphoreType.DMA((copies,)),
            pltpu.SemaphoreType.DMA((copies,)),
        ],
        compiler_params=pltpu.CompilerParams(
            collective_id=0, has_side_effects=True, vmem_limit_bytes=62 * 2**20
        ),
        cost_estimate=pl.CostEstimate(
            flops=4 * slots * bs * bs * ch, bytes_accessed=slots * bs * bs * 2, transcendentals=0
        ),
        name="two_layers",
    )(
        features.reshape(own_blocks, bs, ch),
        block_rows,
        block_cols,
        block_vals.reshape(slots, bs, bs),
        tile_counts,
        w_first,
        b_first.reshape(1, ch),
        w_second,
        b_second.reshape(1, ch),
    )
    return out.reshape(own_blocks * bs, ch)


def solution(mesh):
    in_specs = (
        P(("row", "col"), None),
        P("row", "col", None),
        P("row", "col", None),
        P("row", "col", None, None, None),
        P("row", "col"),
        P(),
        P(),
        P(),
        P(),
    )
    out_specs = P(("row", "col"), None)
    return jax.shard_map(
        per_device, mesh=mesh, in_specs=in_specs, out_specs=out_specs, check_vma=False
    )
```

```python
import functools

import jax
import jax.numpy as jnp
from jax import lax
from jax.experimental import pallas as pl
from jax.experimental.pallas import tpu as pltpu
from jax.sharding import PartitionSpec as P

UNROLL = 176
LOADS = 8
LANES = 128
RING = 4
CUTS_FIRST = (4, 4)
CUTS_MIDDLE = (4, 4)
CUTS_LAST = (4, 4)


def pieces_of(cuts):
    return [(sum(cuts[:i]), size) for i, size in enumerate(cuts)]


def kernel(
    feat,
    rows_hbm,
    cols_hbm,
    vals_hbm,
    count_hbm,
    w1_hbm,
    b1_hbm,
    w2_hbm,
    b2_hbm,
    out_hbm,
    rows_ref,
    cols_ref,
    count_ref,
    w1,
    b1,
    w2,
    b2,
    out_ref,
    vals,
    sums,
    panel_one,
    panel_two,
    send_buf,
    land,
    pad_rows,
    pad_cols,
    list_v,
    list_s,
    small_sem,
    load_sem,
    local_sem,
    send_sem,
    recv_sem,
):
    slots, bs, ch = vals.shape
    panels = (panel_one, panel_two)
    own_blocks = feat.shape[0]
    row_blocks = send_buf.shape[0]
    row = lax.axis_index("row")
    col = lax.axis_index("col")
    zh, y, core = row // 8, (row // 2) % RING, row % 2
    x, zl = col // 2, col % 2

    def row_of(dz, dy, dk):
        return ((zh + dz) % 2) * 8 + ((y + dy + RING) % RING) * 2 + (core + dk) % 2

    def col_of(dx, dl):
        return ((x + dx + RING) % RING) * 2 + (zl + dl) % 2

    yp, ym = (row_of(0, 1, 0), col), (row_of(0, -1, 0), col)
    zp, sib = (row_of(1, 0, 0), col), (row_of(0, 0, 1), col)
    xp, xm, lp = (row, col_of(1, 0)), (row, col_of(-1, 0)), (row, col_of(0, 1))
    y2, x2 = (row_of(0, 2, 0), col), (row, col_of(2, 0))

    small = []
    for src, dst in (
        (count_hbm, count_ref),
        (rows_hbm, rows_ref),
        (cols_hbm, cols_ref),
        (w1_hbm, w1),
        (b1_hbm, b1),
        (w2_hbm, w2),
        (b2_hbm, b2),
    ):
        small.append(pltpu.make_async_copy(src, dst, small_sem.at[len(small)]))
        small[-1].start()
    loads = []
    share = slots // LOADS
    for i in range(LOADS):
        part = pl.ds(i * share, share)
        loads.append(pltpu.make_async_copy(vals_hbm.at[part], vals.at[part], load_sem.at[i]))
        loads[-1].start()
    own_copy = pltpu.make_async_copy(
        feat, panel_one.at[pl.ds(row * own_blocks, own_blocks)], local_sem.at[0]
    )
    own_copy.start()

    barrier = pltpu.get_barrier_semaphore()
    for peer in (yp, ym, zp, sib, xp, xm, lp, y2, x2):
        pl.semaphore_signal(barrier, inc=1, device_id=peer, device_id_type=pl.DeviceIdType.MESH)
    pl.semaphore_wait(barrier, 9)

    started = []

    def send(src, dst, peer):
        i = len(started)
        copy = pltpu.make_async_remote_copy(
            src_ref=src,
            dst_ref=dst,
            send_sem=send_sem.at[i],
            recv_sem=recv_sem.at[i],
            device_id=peer,
            device_id_type=pl.DeviceIdType.MESH,
        )
        copy.start()
        started.append(copy)
        return copy

    def gather_round(layer, piece, own_src):
        def at(who):
            return panels[layer].at[pl.ds(who * own_blocks + piece[0], piece[1])]

        def forward(who, peer):
            return send(at(who), at(who), peer)

        me, mine = row, own_src(piece)
        over = send(mine, at(me), zp)
        far = send(mine, at(me), y2)
        up = send(mine, at(me), yp)
        down = send(mine, at(me), ym)
        shared = [send(mine, at(me), sib)]
        yield
        over.wait_recv()
        over_up = forward(row_of(1, 0, 0), yp)
        over_down = forward(row_of(1, 0, 0), ym)
        shared.append(forward(row_of(1, 0, 0), sib))
        far.wait_recv()
        far_over = forward(row_of(0, 2, 0), zp)
        shared.append(forward(row_of(0, 2, 0), sib))
        yield
        up.wait_recv()
        shared.append(forward(row_of(0, -1, 0), sib))
        down.wait_recv()
        shared.append(forward(row_of(0, 1, 0), sib))
        yield
        over_up.wait_recv()
        shared.append(forward(row_of(1, -1, 0), sib))
        over_down.wait_recv()
        shared.append(forward(row_of(1, 1, 0), sib))
        far_over.wait_recv()
        shared.append(forward(row_of(1, 2, 0), sib))
        yield
        for copy in shared:
            copy.wait_recv()
        yield

    def build_lists():
        tiles = pad_rows.shape[0]
        lane = lax.broadcasted_iota(jnp.int32, (LANES, LANES), 1)
        depth = lax.broadcasted_iota(jnp.int32, (LANES, LANES), 0)
        place = lax.broadcasted_iota(jnp.int32, (1, LANES), 1)
        live_count = count_ref[0, 0]
        for t in range(tiles):
            width = min(LANES, slots - t * LANES)
            if width < LANES:
                pad_rows[t : t + 1, :] = jnp.zeros((1, LANES), jnp.int32)
                pad_cols[t : t + 1, :] = jnp.zeros((1, LANES), jnp.int32)
            pad_rows[t : t + 1, 0:width] = rows_ref[0, :, t * LANES : t * LANES + width]
            pad_cols[t : t + 1, 0:width] = cols_ref[0, :, t * LANES : t * LANES + width]
        key_rows, key_cols, load_cols, group_cols = [], [], [], []

        def upright(v):
            return jnp.sum(jnp.where(lane == depth, v, 0), axis=1, keepdims=True)

        for t in range(tiles):
            index = place + t * LANES
            group = jnp.where(index < live_count, pad_rows[t : t + 1, :], LANES - 1)
            key = group * 1024 + index
            key_rows.append(key)
            key_cols.append(upright(key))
            load_cols.append(upright(index + pad_cols[t : t + 1, :] * 1024 + group * 131072))
            group_cols.append(upright(group))
        ranks = []
        for t in range(tiles):
            below = jnp.zeros((LANES, LANES), jnp.int32)
            for s in range(tiles):
                below = below + (key_rows[s] < key_cols[t]).astype(jnp.int32)
            ranks.append(jnp.sum(below, axis=1, keepdims=True))
        for t in range(tiles):
            found = jnp.zeros((LANES, LANES), jnp.int32)
            for s in range(tiles):
                found = found + jnp.where(ranks[s] == lane + t * LANES, load_cols[s], 0)
            list_v[t : t + 1, :] = jnp.sum(found, axis=0, keepdims=True)
        upto = jnp.zeros((LANES, LANES), jnp.int32)
        for s in range(tiles):
            upto = upto + (group_cols[s] <= lane).astype(jnp.int32)
        list_v[tiles : tiles + 1, :] = jnp.sum(upto, axis=0, keepdims=True)
        for t in range(tiles + 1, list_v.shape[0]):
            list_v[t : t + 1, :] = jnp.zeros((1, LANES), jnp.int32)
        copy = pltpu.make_async_copy(list_v, list_s, local_sem.at[1])
        copy.start()
        copy.wait()

    def multiply(layer):
        def group(g, carry):
            total, last = carry
            for u in range(UNROLL):
                place = g * UNROLL + u
                entry = list_s[place // LANES, place % LANES]
                slot = entry & 1023
                source = (entry >> 10) & 127
                target = entry >> 17
                product = jnp.dot(
                    vals[slot], panels[layer][source], preferred_element_type=jnp.float32
                )
                total = jnp.where(target == last, total, 0.0) + product
                sums[g * UNROLL + u] = total.astype(jnp.bfloat16)
                last = target
            return total, last

        lax.fori_loop(
            0, slots // UNROLL, group, (jnp.zeros((bs, ch), jnp.float32), jnp.int32(-1))
        )

    tiles = pad_rows.shape[0]

    def collect(owner, p):
        for j in range(p[0], p[0] + p[1]):
            r = owner * own_blocks + j
            end = list_s[tiles, r]
            start = jnp.where(r > 0, list_s[tiles, jnp.maximum(r - 1, 0)], 0)
            value = sums[jnp.maximum(end - 1, 0)]
            send_buf[r] = jnp.where(end > start, value, jnp.zeros_like(value))

    def wide(v):
        return v.astype(jnp.float32)

    def scatter(layer, pieces, finish, between, after):
        def part(dx, dl, p):
            return send_buf.at[pl.ds(col_of(dx, dl) * own_blocks + p[0], p[1])]

        def landed(which, p):
            return land.at[layer, which, pl.ds(p[0], p[1])]

        def first(p):
            for dx, dl in ((2, 1), (1, 1), (-1, 1), (2, 0), (1, 0), (-1, 0), (0, 1), (0, 0)):
                collect(col_of(dx, dl), p)
            return (
                send(part(2, 1, p), landed(0, p), lp),
                send(part(1, 1, p), landed(1, p), xp),
                send(part(-1, 1, p), landed(2, p), xm),
                send(part(1, 0, p), landed(3, p), xp),
                send(part(-1, 0, p), landed(4, p), xm),
            )

        def second(p, copies):
            copies[0].wait_recv()
            mine = part(2, 0, p)
            mine[...] = (wide(mine[...]) + wide(landed(0, p)[...])).astype(jnp.bfloat16)
            return copies + (send(mine, landed(5, p), x2),)

        def third(p, copies):
            copies[1].wait_recv()
            copies[2].wait_recv()
            mine = part(0, 1, p)
            total = wide(mine[...]) + wide(landed(1, p)[...]) + wide(landed(2, p)[...])
            mine[...] = total.astype(jnp.bfloat16)
            return copies + (send(mine, landed(6, p), lp),)

        def fourth(p, copies):
            for copy in copies[3:]:
                copy.wait_recv()
            total = wide(part(0, 0, p)[...])
            for which in (3, 4, 5, 6):
                total = total + wide(landed(which, p)[...])
            finish(p, total.astype(jnp.bfloat16).reshape(p[1] * bs, ch))

        state = first(pieces[0])
        for i, p in enumerate(pieces):
            copies = second(p, state)
            if i + 1 < len(pieces):
                state = first(pieces[i + 1])
            copies = third(p, copies)
            between()
            fourth(p, copies)
            after(i)

    rounds = [
        gather_round(0, piece, lambda p: feat.at[pl.ds(p[0], p[1])])
        for piece in pieces_of(CUTS_FIRST)
    ]
    for r in rounds:
        next(r)
    for copy in small:
        copy.wait()
    build_lists()
    for _ in range(4):
        for r in rounds:
            next(r)
    own_copy.wait()
    for copy in loads:
        copy.wait()
    multiply(0)

    middle = pieces_of(CUTS_MIDDLE)
    live = []

    def hidden(p, agg):
        value = jnp.dot(agg, w1[...], preferred_element_type=jnp.float32) + b1[...]
        value = jnp.maximum(value, 0.0).astype(jnp.bfloat16)
        panel_two[pl.ds(row * own_blocks + p[0], p[1])] = value.reshape(p[1], bs, ch)

    def own_hidden(p):
        return panel_two.at[pl.ds(row * own_blocks + p[0], p[1])]

    def step_all():
        for r in list(live):
            if next(r, live) is live:
                live.remove(r)

    def after(i):
        live.append(gather_round(1, middle[i], own_hidden))
        next(live[-1])

    before = len(started)
    scatter(0, middle, hidden, step_all, after)
    while live:
        step_all()
    multiply(1)

    for copy in started[before:]:
        copy.wait_send()

    def final(p, agg):
        value = jnp.dot(agg, w2[...], preferred_element_type=jnp.float32) + b2[...]
        out_ref[p[0] : p[0] + p[1]] = value.astype(jnp.bfloat16).reshape(p[1], bs, ch)
        here = pl.ds(p[0], p[1])
        copy = pltpu.make_async_copy(
            out_ref.at[here], out_hbm.at[here], local_sem.at[2 + len(written)]
        )
        copy.start()
        written.append(copy)

    written = []

    tail = len(started)
    scatter(1, pieces_of(CUTS_LAST), final, lambda: None, lambda i: None)
    for copy in written:
        copy.wait()
    for copy in started[:before] + started[tail:]:
        copy.wait_send()


def count_copies():
    gather, scatter = 16, 7
    return gather * len(CUTS_FIRST + CUTS_MIDDLE) + scatter * len(CUTS_MIDDLE + CUTS_LAST)


def per_device(
    features, block_rows, block_cols, block_vals, tile_counts, w_first, b_first, w_second, b_second
):
    slots, bs = block_vals.shape[2], block_vals.shape[3]
    ch = features.shape[1]
    own_blocks = features.shape[0] // bs
    n_row, n_col = lax.axis_size("row"), lax.axis_size("col")
    panel_blocks = n_row * own_blocks
    row_blocks = n_col * own_blocks
    tiles = -(-slots // LANES)
    bf16 = jnp.bfloat16
    copies = count_copies()
    hbm = pl.BlockSpec(memory_space=pl.ANY)
    out = pl.pallas_call(
        kernel,
        out_shape=jax.ShapeDtypeStruct((own_blocks, bs, ch), bf16),
        in_specs=[hbm] * 9,
        out_specs=hbm,
        scratch_shapes=[
            pltpu.VMEM(block_rows.shape, jnp.int32),
            pltpu.VMEM(block_cols.shape, jnp.int32),
            pltpu.SMEM(tile_counts.shape, jnp.int32),
            pltpu.VMEM(w_first.shape, bf16),
            pltpu.VMEM((1, ch), jnp.float32),
            pltpu.VMEM(w_second.shape, bf16),
            pltpu.VMEM((1, ch), jnp.float32),
            pltpu.VMEM((own_blocks, bs, ch), bf16),
            pltpu.VMEM((slots, bs, bs), bf16),
            pltpu.VMEM((slots, bs, ch), bf16),
            pltpu.VMEM((panel_blocks, bs, ch), bf16),
            pltpu.VMEM((panel_blocks, bs, ch), bf16),
            pltpu.VMEM((row_blocks, bs, ch), bf16),
            pltpu.VMEM((2, 7, own_blocks, bs, ch), bf16),
            pltpu.VMEM((tiles, LANES), jnp.int32),
            pltpu.VMEM((tiles, LANES), jnp.int32),
            pltpu.VMEM((8, LANES), jnp.int32),
            pltpu.SMEM((8, LANES), jnp.int32),
            pltpu.SemaphoreType.DMA((7,)),
            pltpu.SemaphoreType.DMA((LOADS,)),
            pltpu.SemaphoreType.DMA((2 + len(CUTS_LAST),)),
            pltpu.SemaphoreType.DMA((copies,)),
            pltpu.SemaphoreType.DMA((copies,)),
        ],
        compiler_params=pltpu.CompilerParams(
            collective_id=0, has_side_effects=True, vmem_limit_bytes=62 * 2**20
        ),
        cost_estimate=pl.CostEstimate(
            flops=4 * slots * bs * bs * ch, bytes_accessed=slots * bs * bs * 2, transcendentals=0
        ),
        name="two_layers",
    )(
        features.reshape(own_blocks, bs, ch),
        block_rows,
        block_cols,
        block_vals.reshape(slots, bs, bs),
        tile_counts,
        w_first,
        b_first.reshape(1, ch),
        w_second,
        b_second.reshape(1, ch),
    )
    return out.reshape(own_blocks * bs, ch)


def solution(mesh):
    in_specs = (
        P(("row", "col"), None),
        P("row", "col", None),
        P("row", "col", None),
        P("row", "col", None, None, None),
        P("row", "col"),
        P(),
        P(),
        P(),
        P(),
    )
    out_specs = P(("row", "col"), None)
    return jax.shard_map(
        per_device, mesh=mesh, in_specs=in_specs, out_specs=out_specs, check_vma=False
    )
```

```python
import functools

import jax
import jax.numpy as jnp
from jax import lax
from jax.experimental import pallas as pl
from jax.experimental.pallas import tpu as pltpu
from jax.sharding import PartitionSpec as P

UNROLL = 176
LOADS = 8
LANES = 128
RING = 4
CUTS_FIRST = (6, 2)
CUTS_MIDDLE = (4, 4)
CUTS_LAST = (4, 4)


def pieces_of(cuts):
    return [(sum(cuts[:i]), size) for i, size in enumerate(cuts)]


def kernel(
    feat,
    rows_hbm,
    cols_hbm,
    vals_hbm,
    count_hbm,
    w1_hbm,
    b1_hbm,
    w2_hbm,
    b2_hbm,
    out_hbm,
    rows_ref,
    cols_ref,
    count_ref,
    w1,
    b1,
    w2,
    b2,
    out_ref,
    vals,
    sums,
    panel_one,
    panel_two,
    send_buf,
    land,
    pad_rows,
    pad_cols,
    list_v,
    list_s,
    small_sem,
    load_sem,
    local_sem,
    send_sem,
    recv_sem,
):
    slots, bs, ch = vals.shape
    panels = (panel_one, panel_two)
    own_blocks = feat.shape[0]
    row_blocks = send_buf.shape[0]
    row = lax.axis_index("row")
    col = lax.axis_index("col")
    zh, y, core = row // 8, (row // 2) % RING, row % 2
    x, zl = col // 2, col % 2

    def row_of(dz, dy, dk):
        return ((zh + dz) % 2) * 8 + ((y + dy + RING) % RING) * 2 + (core + dk) % 2

    def col_of(dx, dl):
        return ((x + dx + RING) % RING) * 2 + (zl + dl) % 2

    yp, ym = (row_of(0, 1, 0), col), (row_of(0, -1, 0), col)
    zp, sib = (row_of(1, 0, 0), col), (row_of(0, 0, 1), col)
    xp, xm, lp = (row, col_of(1, 0)), (row, col_of(-1, 0)), (row, col_of(0, 1))
    y2, x2 = (row_of(0, 2, 0), col), (row, col_of(2, 0))

    small = []
    for src, dst in (
        (count_hbm, count_ref),
        (rows_hbm, rows_ref),
        (cols_hbm, cols_ref),
        (w1_hbm, w1),
        (b1_hbm, b1),
        (w2_hbm, w2),
        (b2_hbm, b2),
    ):
        small.append(pltpu.make_async_copy(src, dst, small_sem.at[len(small)]))
        small[-1].start()
    loads = []
    share = slots // LOADS
    for i in range(LOADS):
        part = pl.ds(i * share, share)
        loads.append(pltpu.make_async_copy(vals_hbm.at[part], vals.at[part], load_sem.at[i]))
        loads[-1].start()
    own_copy = pltpu.make_async_copy(
        feat, panel_one.at[pl.ds(row * own_blocks, own_blocks)], local_sem.at[0]
    )
    own_copy.start()

    barrier = pltpu.get_barrier_semaphore()
    for peer in (yp, ym, zp, sib, xp, xm, lp, y2, x2):
        pl.semaphore_signal(barrier, inc=1, device_id=peer, device_id_type=pl.DeviceIdType.MESH)
    pl.semaphore_wait(barrier, 9)

    started = []

    def send(src, dst, peer):
        i = len(started)
        copy = pltpu.make_async_remote_copy(
            src_ref=src,
            dst_ref=dst,
            send_sem=send_sem.at[i],
            recv_sem=recv_sem.at[i],
            device_id=peer,
            device_id_type=pl.DeviceIdType.MESH,
        )
        copy.start()
        started.append(copy)
        return copy

    def gather_round(layer, piece, own_src):
        def at(who):
            return panels[layer].at[pl.ds(who * own_blocks + piece[0], piece[1])]

        def forward(who, peer):
            return send(at(who), at(who), peer)

        me, mine = row, own_src(piece)
        over = send(mine, at(me), zp)
        far = send(mine, at(me), y2)
        up = send(mine, at(me), yp)
        down = send(mine, at(me), ym)
        shared = [send(mine, at(me), sib)]
        yield
        over.wait_recv()
        over_up = forward(row_of(1, 0, 0), yp)
        over_down = forward(row_of(1, 0, 0), ym)
        shared.append(forward(row_of(1, 0, 0), sib))
        far.wait_recv()
        far_over = forward(row_of(0, 2, 0), zp)
        shared.append(forward(row_of(0, 2, 0), sib))
        yield
        up.wait_recv()
        shared.append(forward(row_of(0, -1, 0), sib))
        down.wait_recv()
        shared.append(forward(row_of(0, 1, 0), sib))
        yield
        over_up.wait_recv()
        shared.append(forward(row_of(1, -1, 0), sib))
        over_down.wait_recv()
        shared.append(forward(row_of(1, 1, 0), sib))
        far_over.wait_recv()
        shared.append(forward(row_of(1, 2, 0), sib))
        yield
        for copy in shared:
            copy.wait_recv()
        yield

    def build_lists():
        tiles = pad_rows.shape[0]
        lane = lax.broadcasted_iota(jnp.int32, (LANES, LANES), 1)
        depth = lax.broadcasted_iota(jnp.int32, (LANES, LANES), 0)
        place = lax.broadcasted_iota(jnp.int32, (1, LANES), 1)
        live_count = count_ref[0, 0]
        for t in range(tiles):
            width = min(LANES, slots - t * LANES)
            if width < LANES:
                pad_rows[t : t + 1, :] = jnp.zeros((1, LANES), jnp.int32)
                pad_cols[t : t + 1, :] = jnp.zeros((1, LANES), jnp.int32)
            pad_rows[t : t + 1, 0:width] = rows_ref[0, :, t * LANES : t * LANES + width]
            pad_cols[t : t + 1, 0:width] = cols_ref[0, :, t * LANES : t * LANES + width]
        key_rows, key_cols, load_cols, group_cols = [], [], [], []

        def upright(v):
            return jnp.sum(jnp.where(lane == depth, v, 0), axis=1, keepdims=True)

        for t in range(tiles):
            index = place + t * LANES
            group = jnp.where(index < live_count, pad_rows[t : t + 1, :], LANES - 1)
            key = group * 1024 + index
            key_rows.append(key)
            key_cols.append(upright(key))
            load_cols.append(upright(index + pad_cols[t : t + 1, :] * 1024 + group * 131072))
            group_cols.append(upright(group))
        ranks = []
        for t in range(tiles):
            below = jnp.zeros((LANES, LANES), jnp.int32)
            for s in range(tiles):
                below = below + (key_rows[s] < key_cols[t]).astype(jnp.int32)
            ranks.append(jnp.sum(below, axis=1, keepdims=True))
        for t in range(tiles):
            found = jnp.zeros((LANES, LANES), jnp.int32)
            for s in range(tiles):
                found = found + jnp.where(ranks[s] == lane + t * LANES, load_cols[s], 0)
            list_v[t : t + 1, :] = jnp.sum(found, axis=0, keepdims=True)
        upto = jnp.zeros((LANES, LANES), jnp.int32)
        for s in range(tiles):
            upto = upto + (group_cols[s] <= lane).astype(jnp.int32)
        list_v[tiles : tiles + 1, :] = jnp.sum(upto, axis=0, keepdims=True)
        for t in range(tiles + 1, list_v.shape[0]):
            list_v[t : t + 1, :] = jnp.zeros((1, LANES), jnp.int32)
        copy = pltpu.make_async_copy(list_v, list_s, local_sem.at[1])
        copy.start()
        copy.wait()

    def multiply(layer):
        def group(g, carry):
            total, last = carry
            for u in range(UNROLL):
                place = g * UNROLL + u
                entry = list_s[place // LANES, place % LANES]
                slot = entry & 1023
                source = (entry >> 10) & 127
                target = entry >> 17
                product = jnp.dot(
                    vals[slot], panels[layer][source], preferred_element_type=jnp.float32
                )
                total = jnp.where(target == last, total, 0.0) + product
                sums[g * UNROLL + u] = total.astype(jnp.bfloat16)
                last = target
            return total, last

        lax.fori_loop(
            0, slots // UNROLL, group, (jnp.zeros((bs, ch), jnp.float32), jnp.int32(-1))
        )

    tiles = pad_rows.shape[0]

    def collect(owner, p):
        for j in range(p[0], p[0] + p[1]):
            r = owner * own_blocks + j
            end = list_s[tiles, r]
            start = jnp.where(r > 0, list_s[tiles, jnp.maximum(r - 1, 0)], 0)
            value = sums[jnp.maximum(end - 1, 0)]
            send_buf[r] = jnp.where(end > start, value, jnp.zeros_like(value))

    def wide(v):
        return v.astype(jnp.float32)

    def scatter(layer, pieces, finish, between, after):
        def part(dx, dl, p):
            return send_buf.at[pl.ds(col_of(dx, dl) * own_blocks + p[0], p[1])]

        def landed(which, p):
            return land.at[layer, which, pl.ds(p[0], p[1])]

        def first(p):
            copies = []
            for dx, dl, which, peer in (
                (2, 1, 0, lp),
                (1, 1, 1, xp),
                (-1, 1, 2, xm),
                (1, 0, 3, xp),
                (-1, 0, 4, xm),
            ):
                collect(col_of(dx, dl), p)
                copies.append(send(part(dx, dl, p), landed(which, p), peer))
            for dx, dl in ((2, 0), (0, 1), (0, 0)):
                collect(col_of(dx, dl), p)
            return tuple(copies)

        def second(p, copies):
            copies[0].wait_recv()
            mine = part(2, 0, p)
            mine[...] = (wide(mine[...]) + wide(landed(0, p)[...])).astype(jnp.bfloat16)
            return copies + (send(mine, landed(5, p), x2),)

        def third(p, copies):
            copies[1].wait_recv()
            copies[2].wait_recv()
            mine = part(0, 1, p)
            total = wide(mine[...]) + wide(landed(1, p)[...]) + wide(landed(2, p)[...])
            mine[...] = total.astype(jnp.bfloat16)
            return copies + (send(mine, landed(6, p), lp),)

        def fourth(p, copies):
            for copy in copies[3:]:
                copy.wait_recv()
            total = wide(part(0, 0, p)[...])
            for which in (3, 4, 5, 6):
                total = total + wide(landed(which, p)[...])
            finish(p, total.astype(jnp.bfloat16).reshape(p[1] * bs, ch))

        state = first(pieces[0])
        for i, p in enumerate(pieces):
            copies = second(p, state)
            if i + 1 < len(pieces):
                state = first(pieces[i + 1])
            copies = third(p, copies)
            between()
            fourth(p, copies)
            after(i)

    rounds = [
        gather_round(0, piece, lambda p: feat.at[pl.ds(p[0], p[1])])
        for piece in pieces_of(CUTS_FIRST)
    ]
    for r in rounds:
        next(r)
    for copy in small:
        copy.wait()
    build_lists()
    for _ in range(4):
        for r in rounds:
            next(r)
    own_copy.wait()
    for copy in loads:
        copy.wait()
    multiply(0)

    middle = pieces_of(CUTS_MIDDLE)
    live = []

    def hidden(p, agg):
        value = jnp.dot(agg, w1[...], preferred_element_type=jnp.float32) + b1[...]
        value = jnp.maximum(value, 0.0).astype(jnp.bfloat16)
        panel_two[pl.ds(row * own_blocks + p[0], p[1])] = value.reshape(p[1], bs, ch)

    def own_hidden(p):
        return panel_two.at[pl.ds(row * own_blocks + p[0], p[1])]

    def step_all():
        for r in list(live):
            if next(r, live) is live:
                live.remove(r)

    def after(i):
        live.append(gather_round(1, middle[i], own_hidden))
        next(live[-1])

    before = len(started)
    scatter(0, middle, hidden, step_all, after)
    while live:
        step_all()
    multiply(1)

    for copy in started[before:]:
        copy.wait_send()

    def final(p, agg):
        value = jnp.dot(agg, w2[...], preferred_element_type=jnp.float32) + b2[...]
        out_ref[p[0] : p[0] + p[1]] = value.astype(jnp.bfloat16).reshape(p[1], bs, ch)
        here = pl.ds(p[0], p[1])
        copy = pltpu.make_async_copy(
            out_ref.at[here], out_hbm.at[here], local_sem.at[2 + len(written)]
        )
        copy.start()
        written.append(copy)

    written = []

    tail = len(started)
    scatter(1, pieces_of(CUTS_LAST), final, lambda: None, lambda i: None)
    for copy in written:
        copy.wait()
    for copy in started[:before] + started[tail:]:
        copy.wait_send()


def count_copies():
    gather, scatter = 16, 7
    return gather * len(CUTS_FIRST + CUTS_MIDDLE) + scatter * len(CUTS_MIDDLE + CUTS_LAST)


def per_device(
    features, block_rows, block_cols, block_vals, tile_counts, w_first, b_first, w_second, b_second
):
    slots, bs = block_vals.shape[2], block_vals.shape[3]
    ch = features.shape[1]
    own_blocks = features.shape[0] // bs
    n_row, n_col = lax.axis_size("row"), lax.axis_size("col")
    panel_blocks = n_row * own_blocks
    row_blocks = n_col * own_blocks
    tiles = -(-slots // LANES)
    bf16 = jnp.bfloat16
    copies = count_copies()
    hbm = pl.BlockSpec(memory_space=pl.ANY)
    out = pl.pallas_call(
        kernel,
        out_shape=jax.ShapeDtypeStruct((own_blocks, bs, ch), bf16),
        in_specs=[hbm] * 9,
        out_specs=hbm,
        scratch_shapes=[
            pltpu.VMEM(block_rows.shape, jnp.int32),
            pltpu.VMEM(block_cols.shape, jnp.int32),
            pltpu.SMEM(tile_counts.shape, jnp.int32),
            pltpu.VMEM(w_first.shape, bf16),
            pltpu.VMEM((1, ch), jnp.float32),
            pltpu.VMEM(w_second.shape, bf16),
            pltpu.VMEM((1, ch), jnp.float32),
            pltpu.VMEM((own_blocks, bs, ch), bf16),
            pltpu.VMEM((slots, bs, bs), bf16),
            pltpu.VMEM((slots, bs, ch), bf16),
            pltpu.VMEM((panel_blocks, bs, ch), bf16),
            pltpu.VMEM((panel_blocks, bs, ch), bf16),
            pltpu.VMEM((row_blocks, bs, ch), bf16),
            pltpu.VMEM((2, 7, own_blocks, bs, ch), bf16),
            pltpu.VMEM((tiles, LANES), jnp.int32),
            pltpu.VMEM((tiles, LANES), jnp.int32),
            pltpu.VMEM((8, LANES), jnp.int32),
            pltpu.SMEM((8, LANES), jnp.int32),
            pltpu.SemaphoreType.DMA((7,)),
            pltpu.SemaphoreType.DMA((LOADS,)),
            pltpu.SemaphoreType.DMA((2 + len(CUTS_LAST),)),
            pltpu.SemaphoreType.DMA((copies,)),
            pltpu.SemaphoreType.DMA((copies,)),
        ],
        compiler_params=pltpu.CompilerParams(
            collective_id=0, has_side_effects=True, vmem_limit_bytes=62 * 2**20
        ),
        cost_estimate=pl.CostEstimate(
            flops=4 * slots * bs * bs * ch, bytes_accessed=slots * bs * bs * 2, transcendentals=0
        ),
        name="two_layers",
    )(
        features.reshape(own_blocks, bs, ch),
        block_rows,
        block_cols,
        block_vals.reshape(slots, bs, bs),
        tile_counts,
        w_first,
        b_first.reshape(1, ch),
        w_second,
        b_second.reshape(1, ch),
    )
    return out.reshape(own_blocks * bs, ch)


def solution(mesh):
    in_specs = (
        P(("row", "col"), None),
        P("row", "col", None),
        P("row", "col", None),
        P("row", "col", None, None, None),
        P("row", "col"),
        P(),
        P(),
        P(),
        P(),
    )
    out_specs = P(("row", "col"), None)
    return jax.shard_map(
        per_device, mesh=mesh, in_specs=in_specs, out_specs=out_specs, check_vma=False
    )
```

```python
import functools

import jax
import jax.numpy as jnp
from jax import lax
from jax.experimental import pallas as pl
from jax.experimental.pallas import tpu as pltpu
from jax.sharding import PartitionSpec as P

UNROLL = 352
LOADS = 8
LANES = 128
RING = 4
CUTS_FIRST = (6, 2)
CUTS_MIDDLE = (4, 4)
CUTS_LAST = (4, 4)


def pieces_of(cuts):
    return [(sum(cuts[:i]), size) for i, size in enumerate(cuts)]


def kernel(
    feat,
    rows_hbm,
    cols_hbm,
    vals_hbm,
    count_hbm,
    w1_hbm,
    b1_hbm,
    w2_hbm,
    b2_hbm,
    out_hbm,
    rows_ref,
    cols_ref,
    count_ref,
    w1,
    b1,
    w2,
    b2,
    out_ref,
    vals,
    sums,
    panel_one,
    panel_two,
    send_buf,
    land,
    pad_rows,
    pad_cols,
    list_v,
    list_s,
    small_sem,
    load_sem,
    local_sem,
    send_sem,
    recv_sem,
):
    slots, bs, ch = vals.shape
    panels = (panel_one, panel_two)
    own_blocks = feat.shape[0]
    row_blocks = send_buf.shape[0]
    row = lax.axis_index("row")
    col = lax.axis_index("col")
    zh, y, core = row // 8, (row // 2) % RING, row % 2
    x, zl = col // 2, col % 2

    def row_of(dz, dy, dk):
        return ((zh + dz) % 2) * 8 + ((y + dy + RING) % RING) * 2 + (core + dk) % 2

    def col_of(dx, dl):
        return ((x + dx + RING) % RING) * 2 + (zl + dl) % 2

    yp, ym = (row_of(0, 1, 0), col), (row_of(0, -1, 0), col)
    zp, sib = (row_of(1, 0, 0), col), (row_of(0, 0, 1), col)
    xp, xm, lp = (row, col_of(1, 0)), (row, col_of(-1, 0)), (row, col_of(0, 1))
    y2, x2 = (row_of(0, 2, 0), col), (row, col_of(2, 0))

    barrier = pltpu.get_barrier_semaphore()
    for peer in (yp, ym, zp, sib, xp, xm, lp, y2, x2):
        pl.semaphore_signal(barrier, inc=1, device_id=peer, device_id_type=pl.DeviceIdType.MESH)
    small = []
    for src, dst in (
        (count_hbm, count_ref),
        (rows_hbm, rows_ref),
        (cols_hbm, cols_ref),
        (w1_hbm, w1),
        (b1_hbm, b1),
        (w2_hbm, w2),
        (b2_hbm, b2),
    ):
        small.append(pltpu.make_async_copy(src, dst, small_sem.at[len(small)]))
        small[-1].start()
    loads = []
    share = slots // LOADS
    for i in range(LOADS):
        part = pl.ds(i * share, share)
        loads.append(pltpu.make_async_copy(vals_hbm.at[part], vals.at[part], load_sem.at[i]))
        loads[-1].start()
    own_copy = pltpu.make_async_copy(
        feat, panel_one.at[pl.ds(row * own_blocks, own_blocks)], local_sem.at[0]
    )
    own_copy.start()

    pl.semaphore_wait(barrier, 9)

    started = []

    def send(src, dst, peer):
        i = len(started)
        copy = pltpu.make_async_remote_copy(
            src_ref=src,
            dst_ref=dst,
            send_sem=send_sem.at[i],
            recv_sem=recv_sem.at[i],
            device_id=peer,
            device_id_type=pl.DeviceIdType.MESH,
        )
        copy.start()
        started.append(copy)
        return copy

    def gather_round(layer, piece, own_src):
        def at(who):
            return panels[layer].at[pl.ds(who * own_blocks + piece[0], piece[1])]

        def forward(who, peer):
            return send(at(who), at(who), peer)

        me, mine = row, own_src(piece)
        over = send(mine, at(me), zp)
        far = send(mine, at(me), y2)
        up = send(mine, at(me), yp)
        down = send(mine, at(me), ym)
        shared = [send(mine, at(me), sib)]
        yield
        over.wait_recv()
        over_up = forward(row_of(1, 0, 0), yp)
        over_down = forward(row_of(1, 0, 0), ym)
        shared.append(forward(row_of(1, 0, 0), sib))
        far.wait_recv()
        far_over = forward(row_of(0, 2, 0), zp)
        shared.append(forward(row_of(0, 2, 0), sib))
        yield
        up.wait_recv()
        shared.append(forward(row_of(0, -1, 0), sib))
        down.wait_recv()
        shared.append(forward(row_of(0, 1, 0), sib))
        yield
        over_up.wait_recv()
        shared.append(forward(row_of(1, -1, 0), sib))
        over_down.wait_recv()
        shared.append(forward(row_of(1, 1, 0), sib))
        far_over.wait_recv()
        shared.append(forward(row_of(1, 2, 0), sib))
        yield
        for copy in shared:
            copy.wait_recv()
        yield

    def build_lists():
        tiles = pad_rows.shape[0]
        lane = lax.broadcasted_iota(jnp.int32, (LANES, LANES), 1)
        depth = lax.broadcasted_iota(jnp.int32, (LANES, LANES), 0)
        place = lax.broadcasted_iota(jnp.int32, (1, LANES), 1)
        live_count = count_ref[0, 0]
        for t in range(tiles):
            width = min(LANES, slots - t * LANES)
            if width < LANES:
                pad_rows[t : t + 1, :] = jnp.zeros((1, LANES), jnp.int32)
                pad_cols[t : t + 1, :] = jnp.zeros((1, LANES), jnp.int32)
            pad_rows[t : t + 1, 0:width] = rows_ref[0, :, t * LANES : t * LANES + width]
            pad_cols[t : t + 1, 0:width] = cols_ref[0, :, t * LANES : t * LANES + width]
        key_rows, key_cols, load_cols, group_cols = [], [], [], []

        def upright(v):
            return jnp.sum(jnp.where(lane == depth, v, 0), axis=1, keepdims=True)

        for t in range(tiles):
            index = place + t * LANES
            group = jnp.where(index < live_count, pad_rows[t : t + 1, :], LANES - 1)
            key = group * 1024 + index
            key_rows.append(key)
            key_cols.append(upright(key))
            load_cols.append(upright(index + pad_cols[t : t + 1, :] * 1024 + group * 131072))
            group_cols.append(upright(group))
        ranks = []
        for t in range(tiles):
            below = jnp.zeros((LANES, LANES), jnp.int32)
            for s in range(tiles):
                below = below + (key_rows[s] < key_cols[t]).astype(jnp.int32)
            ranks.append(jnp.sum(below, axis=1, keepdims=True))
        for t in range(tiles):
            found = jnp.zeros((LANES, LANES), jnp.int32)
            for s in range(tiles):
                found = found + jnp.where(ranks[s] == lane + t * LANES, load_cols[s], 0)
            list_v[t : t + 1, :] = jnp.sum(found, axis=0, keepdims=True)
        upto = jnp.zeros((LANES, LANES), jnp.int32)
        for s in range(tiles):
            upto = upto + (group_cols[s] <= lane).astype(jnp.int32)
        list_v[tiles : tiles + 1, :] = jnp.sum(upto, axis=0, keepdims=True)
        for t in range(tiles + 1, list_v.shape[0]):
            list_v[t : t + 1, :] = jnp.zeros((1, LANES), jnp.int32)
        copy = pltpu.make_async_copy(list_v, list_s, local_sem.at[1])
        copy.start()
        copy.wait()

    def multiply(layer):
        def group(g, carry):
            total, last = carry
            for u in range(UNROLL):
                place = g * UNROLL + u
                entry = list_s[place // LANES, place % LANES]
                slot = entry & 1023
                source = (entry >> 10) & 127
                target = entry >> 17
                product = jnp.dot(
                    vals[slot], panels[layer][source], preferred_element_type=jnp.float32
                )
                total = jnp.where(target == last, total, 0.0) + product
                sums[g * UNROLL + u] = total.astype(jnp.bfloat16)
                last = target
            return total, last

        lax.fori_loop(
            0, slots // UNROLL, group, (jnp.zeros((bs, ch), jnp.float32), jnp.int32(-1))
        )

    tiles = pad_rows.shape[0]

    def collect(owner, p):
        for j in range(p[0], p[0] + p[1]):
            r = owner * own_blocks + j
            end = list_s[tiles, r]
            start = jnp.where(r > 0, list_s[tiles, jnp.maximum(r - 1, 0)], 0)
            value = sums[jnp.maximum(end - 1, 0)]
            send_buf[r] = jnp.where(end > start, value, jnp.zeros_like(value))

    def wide(v):
        return v.astype(jnp.float32)

    def scatter(layer, pieces, finish, between, after):
        def part(dx, dl, p):
            return send_buf.at[pl.ds(col_of(dx, dl) * own_blocks + p[0], p[1])]

        def landed(which, p):
            return land.at[layer, which, pl.ds(p[0], p[1])]

        def first(p):
            copies = []
            for dx, dl, which, peer in (
                (2, 1, 0, lp),
                (1, 1, 1, xp),
                (-1, 1, 2, xm),
                (1, 0, 3, xp),
                (-1, 0, 4, xm),
            ):
                collect(col_of(dx, dl), p)
                copies.append(send(part(dx, dl, p), landed(which, p), peer))
            for dx, dl in ((2, 0), (0, 1), (0, 0)):
                collect(col_of(dx, dl), p)
            return tuple(copies)

        def second(p, copies):
            copies[0].wait_recv()
            mine = part(2, 0, p)
            mine[...] = (wide(mine[...]) + wide(landed(0, p)[...])).astype(jnp.bfloat16)
            return copies + (send(mine, landed(5, p), x2),)

        def third(p, copies):
            copies[1].wait_recv()
            copies[2].wait_recv()
            mine = part(0, 1, p)
            total = wide(mine[...]) + wide(landed(1, p)[...]) + wide(landed(2, p)[...])
            mine[...] = total.astype(jnp.bfloat16)
            return copies + (send(mine, landed(6, p), lp),)

        def fourth(p, copies):
            for copy in copies[3:]:
                copy.wait_recv()
            total = wide(part(0, 0, p)[...])
            for which in (3, 4, 5, 6):
                total = total + wide(landed(which, p)[...])
            finish(p, total.astype(jnp.bfloat16).reshape(p[1] * bs, ch))

        state = first(pieces[0])
        for i, p in enumerate(pieces):
            copies = second(p, state)
            if i + 1 < len(pieces):
                state = first(pieces[i + 1])
            copies = third(p, copies)
            between()
            fourth(p, copies)
            after(i)

    rounds = [
        gather_round(0, piece, lambda p: feat.at[pl.ds(p[0], p[1])])
        for piece in pieces_of(CUTS_FIRST)
    ]
    for r in rounds:
        next(r)
    for copy in small:
        copy.wait()
    build_lists()
    for _ in range(4):
        for r in rounds:
            next(r)
    own_copy.wait()
    for copy in loads:
        copy.wait()
    multiply(0)

    middle = pieces_of(CUTS_MIDDLE)
    live = []

    def hidden(p, agg):
        value = jnp.dot(agg, w1[...], preferred_element_type=jnp.float32) + b1[...]
        value = jnp.maximum(value, 0.0).astype(jnp.bfloat16)
        panel_two[pl.ds(row * own_blocks + p[0], p[1])] = value.reshape(p[1], bs, ch)

    def own_hidden(p):
        return panel_two.at[pl.ds(row * own_blocks + p[0], p[1])]

    def step_all():
        for r in list(live):
            if next(r, live) is live:
                live.remove(r)

    def after(i):
        live.append(gather_round(1, middle[i], own_hidden))
        next(live[-1])

    before = len(started)
    scatter(0, middle, hidden, step_all, after)
    while live:
        step_all()
    multiply(1)

    for copy in started[before:]:
        copy.wait_send()

    def final(p, agg):
        value = jnp.dot(agg, w2[...], preferred_element_type=jnp.float32) + b2[...]
        out_ref[p[0] : p[0] + p[1]] = value.astype(jnp.bfloat16).reshape(p[1], bs, ch)
        here = pl.ds(p[0], p[1])
        copy = pltpu.make_async_copy(
            out_ref.at[here], out_hbm.at[here], local_sem.at[2 + len(written)]
        )
        copy.start()
        written.append(copy)

    written = []

    tail = len(started)
    scatter(1, pieces_of(CUTS_LAST), final, lambda: None, lambda i: None)
    for copy in written:
        copy.wait()
    for copy in started[:before] + started[tail:]:
        copy.wait_send()


def count_copies():
    gather, scatter = 16, 7
    return gather * len(CUTS_FIRST + CUTS_MIDDLE) + scatter * len(CUTS_MIDDLE + CUTS_LAST)


def per_device(
    features, block_rows, block_cols, block_vals, tile_counts, w_first, b_first, w_second, b_second
):
    slots, bs = block_vals.shape[2], block_vals.shape[3]
    ch = features.shape[1]
    own_blocks = features.shape[0] // bs
    n_row, n_col = lax.axis_size("row"), lax.axis_size("col")
    panel_blocks = n_row * own_blocks
    row_blocks = n_col * own_blocks
    tiles = -(-slots // LANES)
    bf16 = jnp.bfloat16
    copies = count_copies()
    hbm = pl.BlockSpec(memory_space=pl.ANY)
    out = pl.pallas_call(
        kernel,
        out_shape=jax.ShapeDtypeStruct((own_blocks, bs, ch), bf16),
        in_specs=[hbm] * 9,
        out_specs=hbm,
        scratch_shapes=[
            pltpu.VMEM(block_rows.shape, jnp.int32),
            pltpu.VMEM(block_cols.shape, jnp.int32),
            pltpu.SMEM(tile_counts.shape, jnp.int32),
            pltpu.VMEM(w_first.shape, bf16),
            pltpu.VMEM((1, ch), jnp.float32),
            pltpu.VMEM(w_second.shape, bf16),
            pltpu.VMEM((1, ch), jnp.float32),
            pltpu.VMEM((own_blocks, bs, ch), bf16),
            pltpu.VMEM((slots, bs, bs), bf16),
            pltpu.VMEM((slots, bs, ch), bf16),
            pltpu.VMEM((panel_blocks, bs, ch), bf16),
            pltpu.VMEM((panel_blocks, bs, ch), bf16),
            pltpu.VMEM((row_blocks, bs, ch), bf16),
            pltpu.VMEM((2, 7, own_blocks, bs, ch), bf16),
            pltpu.VMEM((tiles, LANES), jnp.int32),
            pltpu.VMEM((tiles, LANES), jnp.int32),
            pltpu.VMEM((8, LANES), jnp.int32),
            pltpu.SMEM((8, LANES), jnp.int32),
            pltpu.SemaphoreType.DMA((7,)),
            pltpu.SemaphoreType.DMA((LOADS,)),
            pltpu.SemaphoreType.DMA((2 + len(CUTS_LAST),)),
            pltpu.SemaphoreType.DMA((copies,)),
            pltpu.SemaphoreType.DMA((copies,)),
        ],
        compiler_params=pltpu.CompilerParams(
            collective_id=0, has_side_effects=True, vmem_limit_bytes=62 * 2**20
        ),
        cost_estimate=pl.CostEstimate(
            flops=4 * slots * bs * bs * ch, bytes_accessed=slots * bs * bs * 2, transcendentals=0
        ),
        name="two_layers",
    )(
        features.reshape(own_blocks, bs, ch),
        block_rows,
        block_cols,
        block_vals.reshape(slots, bs, bs),
        tile_counts,
        w_first,
        b_first.reshape(1, ch),
        w_second,
        b_second.reshape(1, ch),
    )
    return out.reshape(own_blocks * bs, ch)


def solution(mesh):
    in_specs = (
        P(("row", "col"), None),
        P("row", "col", None),
        P("row", "col", None),
        P("row", "col", None, None, None),
        P("row", "col"),
        P(),
        P(),
        P(),
        P(),
    )
    out_specs = P(("row", "col"), None)
    return jax.shard_map(
        per_device, mesh=mesh, in_specs=in_specs, out_specs=out_specs, check_vma=False
    )
```
